256 devices in a mesh: row: 16 (over y, x), col: 16 (over z, core).
Axes of the slice: x: 4, y: 4, z: 8, core: 2. Of those that a mesh axis runs over, the one named last changes fastest.
Arguments:
- hist_corr: float32 [16384, 16384], P('row', 'col'), may hold values from -1 to 1
- hist_resp: float32 [16384, 16384], P('row', 'col'), may hold values from -1 to 1, as said below
- row_corr: float32 [128, 16384], P(None, 'col'), may hold values from -1 to 1
- row_resp: float32 [128, 16384], P(None, 'col'), may hold values from -1 to 1
Outputs:
- final_corr: float32 [128, 16384], P(None, 'col')
- final_resp: float32 [128, 16384], P(None, 'col')
The draws below stay inside these ranges and needn't reach their ends.
Inputs may be any that keep to these rules, and one draw needn't show every extreme that they name: hist_resp[s, u] is 0 where u > s and 1 where u == s.
All inputs are finite; a program needn't handle non-finite values.
Results may differ from the reference program's by a relative error of at most 0.00015.
Values sent between devices are 32-bit elements; how exact they have to be, the bound alone decides.
No kernel may reach another device: no remote copies, remote signals or barrier semaphores. Data moves between devices by JAX's collectives and lax.ppermute only.
A program may use at most 64 MiB of HBM per device.

```python
import math
import jax
import jax.numpy as jnp
from jax import lax

HIST = 16384
ROWS = 128
BLOCKS = 4


def draw_hist_corr(key, part):
    base_key = jax.random.fold_in(key, 101)
    rough_part = jax.random.uniform(base_key, (HIST, HIST), jnp.float32, -1.0, 1.0)
    return rough_part


def draw_hist_resp(key, part):
    base_key = jax.random.fold_in(key, 202)
    rough_part = jax.random.uniform(base_key, (HIST, HIST), jnp.float32, -1.0, 1.0)
    time_index = jnp.arange(HIST, dtype=jnp.int32)
    later_mask = time_index[:, None] > time_index[None, :]
    diagonal_mask = time_index[:, None] == time_index[None, :]
    filled = jnp.where(diagonal_mask, jnp.float32(1.0), jnp.float32(0.0))
    return jnp.where(later_mask, rough_part, filled).astype(jnp.float32)


def draw_rows(key, salt_value):
    base_key = jax.random.fold_in(key, salt_value)
    time_grid = jnp.arange(HIST, dtype=jnp.int32).astype(jnp.float32) / HIST
    rough_part = jax.random.uniform(base_key, (ROWS, HIST), jnp.float32, -1.0, 1.0)
    return rough_part * (0.55 + 0.45 * time_grid)[None, :]


def draw_row_corr(key, part):
    return draw_rows(key, 303)


def draw_row_resp(key, part):
    return draw_rows(key, 404)


def setup_inputs(seed: int = 0) -> dict:
    splits = jax.random.split(jax.random.key(seed), 5)
    hist_corr = draw_hist_corr(jax.random.fold_in(splits[4], 71), 0)
    hist_resp = draw_hist_resp(jax.random.fold_in(splits[4], 71), 0)
    row_corr = draw_row_corr(jax.random.fold_in(splits[4], 71), 0)
    row_resp = draw_row_resp(jax.random.fold_in(splits[4], 71), 0)
    return {"hist_corr": hist_corr, "hist_resp": hist_resp, "row_corr": row_corr, "row_resp": row_resp}


step_size = 0.2
heat_reservoir_warmth = 0.6

def reference(hist_corr, hist_resp, row_corr, row_resp):
    highest = lax.Precision.HIGHEST
    integration_coefficient = 1.0 / math.sqrt(HIST)
    autocovariance_curve = row_corr
    perturbation_reaction = row_resp
    for block_index in range(BLOCKS):
        history_integrand = 3.0 * autocovariance_curve * perturbation_reaction
        slope_contribution = 1.5 * autocovariance_curve * autocovariance_curve
        norm_enforcing_scalar = heat_reservoir_warmth + integration_coefficient * lax.optimization_barrier(jnp.sum(history_integrand * autocovariance_curve + slope_contribution * perturbation_reaction, axis=1, keepdims=True))
        memory_corr = jnp.dot(history_integrand, hist_corr, precision=highest, preferred_element_type=jnp.float32)
        memory_resp = jnp.dot(history_integrand, hist_resp, precision=highest, preferred_element_type=jnp.float32)
        memory_cross = lax.dot_general(slope_contribution, hist_resp, (((1,), (1,)), ((), ())), precision=highest, preferred_element_type=jnp.float32)
        next_corr = autocovariance_curve + step_size * (integration_coefficient * (memory_corr + memory_cross) - norm_enforcing_scalar * autocovariance_curve)
        next_resp = perturbation_reaction + step_size * (integration_coefficient * memory_resp - norm_enforcing_scalar * perturbation_reaction)
        autocovariance_curve = next_corr
        perturbation_reaction = next_resp
    return (autocovariance_curve, perturbation_reaction)
```

```python
import functools
import math

import jax
import jax.numpy as jnp
from jax import lax
from jax.experimental import pallas as pl
from jax.experimental.pallas import tpu as pltpu
from jax.sharding import Mesh
from jax.sharding import PartitionSpec as P

HIST = 16384
BLOCKS = 4
SIDE = 16
SLICE = 8
ROWS = SIDE * SLICE
WIDTH = 1024
LANES = 128
TILE = 256
COEFFICIENT = 1.0 / math.sqrt(HIST)

step_size = 0.2
heat_reservoir_warmth = 0.6

ROW = ("y", "x")
ALL = ("y", "x", "z", "core")
TRANSPOSE = [(r * SIDE + c, c * SIDE + r) for r in range(SIDE) for c in range(SIDE)]

f32, bf16 = jnp.float32, jnp.bfloat16


def kernel_call(body, outs, args, scratch=(), flops=0, prefetch=0):
    vmem = pl.BlockSpec(memory_space=pltpu.VMEM)
    smem = pl.BlockSpec(memory_space=pltpu.SMEM)
    size = sum(a.size * a.dtype.itemsize for a in args)
    return pl.pallas_call(
        body,
        out_shape=outs,
        in_specs=[smem] * prefetch + [vmem] * (len(args) - prefetch),
        out_specs=jax.tree.map(lambda _: vmem, outs),
        scratch_shapes=list(scratch),
        compiler_params=pltpu.CompilerParams(vmem_limit_bytes=40 * 1024 * 1024),
        cost_estimate=pl.CostEstimate(flops=flops, bytes_accessed=size, transcendentals=0),
    )(*args)


def shape(*dims, dtype=f32):
    return jax.ShapeDtypeStruct(dims, dtype)


def split(values):
    high = values.astype(bf16)
    low = (values - high.astype(f32)).astype(bf16)
    return high, low


def split_kernel(corr_ref, resp_ref, ch_ref, cl_ref, rh_ref, rl_ref):
    @pl.loop(0, WIDTH // LANES)
    def _(i):
        rows = pl.ds(pl.multiple_of(i * LANES, LANES), LANES)
        ch_ref[rows, :], cl_ref[rows, :] = split(corr_ref[rows, :])
        rh_ref[rows, :], rl_ref[rows, :] = split(resp_ref[rows, :])


def split_history(hist_corr, hist_resp):
    out = shape(WIDTH, WIDTH, dtype=bf16)
    return kernel_call(split_kernel, (out,) * 4, (hist_corr, hist_resp), flops=WIDTH * WIDTH)


def cross_kernel(col_ref, full_ref, rh_ref, rl_ref, keep_ref, give_ref, lhs_ref):
    col = col_ref[0]
    full = full_ref[...].reshape(ROWS, WIDTH)
    lhs_ref[:ROWS], lhs_ref[ROWS:] = split(1.5 * full * full)
    dims = (((1,), (1,)), ((), ()))

    @pl.loop(0, WIDTH // TILE)
    def _(n):
        at = pl.ds(pl.multiple_of(n * TILE, TILE), TILE)
        both = lax.dot_general(lhs_ref[...], rh_ref[at, :], dims, preferred_element_type=f32)
        low = lax.dot_general(lhs_ref[:ROWS], rl_ref[at, :], dims, preferred_element_type=f32)
        total = (both[:ROWS] + (both[ROWS:] + low)).reshape(SIDE, SLICE, TILE)
        for j in range(SIDE):
            slot = j ^ col
            half = slot // 2

            @pl.when(slot % 2 == 0)
            def _():
                keep_ref[half, :, at] = total[j]

            @pl.when(slot % 2 == 1)
            def _():
                give_ref[half, :, at] = total[j]


def cross_parts(col, full, resp_high, resp_low):
    out = shape(SIDE // 2, SLICE, WIDTH)
    return kernel_call(
        cross_kernel,
        (out, out),
        (col, full, resp_high, resp_low),
        scratch=(pltpu.VMEM((2 * ROWS, WIDTH), bf16),),
        flops=6 * ROWS * WIDTH * WIDTH,
        prefetch=1,
    )


def memory_kernel(
    core_ref, mine_ref, other_ref, ch_ref, cl_ref, rh_ref, rl_ref, out_ref, lhs_ref
):
    core = core_ref[0]
    half = ROWS // 2
    for k, ref in enumerate((mine_ref, other_ref)):
        values = ref[:, :, :WIDTH].reshape(half, WIDTH)
        at = pl.ds(k * half, half)
        high, low = split(values)
        lhs_ref[k * half : (k + 1) * half] = high
        lhs_ref[ROWS + k * half : ROWS + (k + 1) * half] = low
        for z in range(SIDE // 2):
            out_ref[2 * z + (core + k) % 2, :, 2 * WIDTH :] = ref[z, :, WIDTH:]
    for first, high_ref, low_ref in ((0, ch_ref, cl_ref), (WIDTH, rh_ref, rl_ref)):

        @pl.loop(0, WIDTH // TILE)
        def _(n):
            at = pl.ds(pl.multiple_of(n * TILE, TILE), TILE)
            to = pl.ds(pl.multiple_of(first + n * TILE, TILE), TILE)
            both = jnp.dot(lhs_ref[...], high_ref[:, at], preferred_element_type=f32)
            low = jnp.dot(lhs_ref[:ROWS], low_ref[:, at], preferred_element_type=f32)
            total = (both[:ROWS] + (both[ROWS:] + low)).reshape(2, SIDE // 2, SLICE, TILE)
            for k in range(2):
                for z in range(SIDE // 2):
                    out_ref[2 * z + (core + k) % 2, :, to] = total[k, z]


def memory_parts(core, mine, other, corr_high, corr_low, resp_high, resp_low):
    return kernel_call(
        memory_kernel,
        shape(SIDE, SLICE, 2 * WIDTH + LANES),
        (core, mine, other, corr_high, corr_low, resp_high, resp_low),
        scratch=(pltpu.VMEM((2 * ROWS, WIDTH), bf16),),
        flops=12 * ROWS * WIDTH * WIDTH,
        prefetch=1,
    )


def energy_message(corr, resp):
    energy = 3.0 * corr * resp
    slope = 1.5 * corr * corr
    terms = jnp.sum(energy * corr + slope * resp, axis=1, keepdims=True)
    return jnp.concatenate([energy, jnp.broadcast_to(terms, (SLICE, LANES))], axis=1)


def advance(pieces, cross, corr, resp):
    sums = jnp.sum(pieces, axis=0)
    memory_corr = sums[:, :WIDTH]
    memory_resp = sums[:, WIDTH : 2 * WIDTH]
    multiplier = heat_reservoir_warmth + COEFFICIENT * sums[:, 2 * WIDTH : 2 * WIDTH + 1]
    return (
        corr + step_size * (COEFFICIENT * (memory_corr + cross) - multiplier * corr),
        resp + step_size * (COEFFICIENT * memory_resp - multiplier * resp),
    )


def advance_kernel(pieces_ref, cross_ref, corr_ref, resp_ref, c_ref, r_ref, m_ref, copies_ref):
    corr, resp = advance(pieces_ref[...], cross_ref[...], corr_ref[...], resp_ref[...])
    c_ref[...] = corr
    r_ref[...] = resp
    m_ref[...] = energy_message(corr, resp)
    for j in range(SIDE):
        copies_ref[j] = corr


def last_kernel(pieces_ref, cross_ref, corr_ref, resp_ref, copies_ref):
    corr, resp = advance(pieces_ref[...], cross_ref[...], corr_ref[...], resp_ref[...])
    for j in range(SIDE):
        copies_ref[j, :, :WIDTH] = corr
        copies_ref[j, :, WIDTH:] = resp


def swap(values, axis, size, bit):
    return lax.ppermute(values, axis, [(i, i ^ bit) for i in range(size)])


def sum_over_col(keep, give):
    total = keep + swap(give, "core", 2, 1)
    for bit in (1, 2, 4):
        pairs = total.reshape(-1, 2, SLICE, WIDTH)
        total = pairs[:, 0] + swap(pairs[:, 1], "z", 8, bit)
    return total[0]


def transpose(piece):
    return lax.ppermute(piece, ALL, TRANSPOSE)


def body(hist_corr, hist_resp, row_corr, row_resp):
    my_row = lax.axis_index(ROW)
    core = lax.axis_index("core")
    col = (2 * lax.axis_index("z") + core).reshape(1)
    core = core.reshape(1)
    corr = lax.dynamic_slice_in_dim(row_corr, my_row * SLICE, SLICE, 0)
    resp = lax.dynamic_slice_in_dim(row_resp, my_row * SLICE, SLICE, 0)
    message = energy_message(corr, resp)
    full = row_corr.reshape(SIDE, SLICE, WIDTH)
    corr_high, corr_low, resp_high, resp_low = split_history(hist_corr, hist_resp)
    for block_index in range(BLOCKS):
        if block_index:
            full = lax.all_to_all(copies, ROW, 0, 0, tiled=True)
        message = transpose(message)
        mine = lax.all_to_all(
            jnp.broadcast_to(message[None], (SIDE // 2,) + message.shape), "z", 0, 0, tiled=True
        )
        other = swap(mine, "core", 2, 1)
        keep, give = cross_parts(col, full, resp_high, resp_low)
        cross = transpose(sum_over_col(keep, give))
        parts = memory_parts(core, mine, other, corr_high, corr_low, resp_high, resp_low)
        pieces = lax.all_to_all(parts, ROW, 0, 0, tiled=True)
        piece = shape(SLICE, WIDTH)
        if block_index < BLOCKS - 1:
            corr, resp, message, copies = kernel_call(
                advance_kernel,
                (piece, piece, shape(SLICE, WIDTH + LANES), shape(SIDE, SLICE, WIDTH)),
                (pieces, cross, corr, resp),
            )
        else:
            copies = kernel_call(
                last_kernel, shape(SIDE, SLICE, 2 * WIDTH), (pieces, cross, corr, resp)
            )
    final = lax.all_to_all(copies, ROW, 0, 0, tiled=True).reshape(ROWS, 2 * WIDTH)
    return (final[:, :WIDTH], final[:, WIDTH:])


def solution(mesh):
    split_mesh = Mesh(mesh.devices.reshape(4, 4, 8, 2), ALL)
    times = ("z", "core")
    in_specs = (P(ROW, times), P(ROW, times), P(None, times), P(None, times))
    out_specs = (P(None, times), P(None, times))
    return jax.shard_map(
        body, mesh=split_mesh, in_specs=in_specs, out_specs=out_specs, check_vma=False
    )
```

```python
import functools
import math

import jax
import jax.numpy as jnp
import numpy as np
from jax import lax
from jax.experimental import pallas as pl
from jax.experimental.pallas import tpu as pltpu
from jax.sharding import Mesh
from jax.sharding import PartitionSpec as P

HIST = 16384
BLOCKS = 4
SIDE = 16
SLICE = 8
ROWS = SIDE * SLICE
WIDTH = 1024
LANES = 128
TILE = 256
COEFFICIENT = 1.0 / math.sqrt(HIST)

step_size = 0.2
heat_reservoir_warmth = 0.6

ROW = ("y", "x")
ALL = ("y", "x", "z", "core")


def around(a, b, size):
    return min((a - b) % size, (b - a) % size)


def pairs_of(b):
    def plane(i):
        return around(i // 4, b // 4, 4) + around(i % 4, b % 4, 4)

    rows = sorted(range(SIDE), key=lambda i: (-plane(i), i))
    cols = sorted(range(SIDE), key=lambda j: (around(j // 2, b // 2, 8), j))
    return dict(zip(rows, cols))


PAIRS = [pairs_of(b) for b in range(SIDE)]
KEPT = np.array([[PAIRS[b][i] for i in range(SIDE)] for b in range(SIDE)], np.int32)
KEEPER = np.argsort(KEPT, axis=1).astype(np.int32)
TO_LINE = [(i * SIDE + b, b * SIDE + int(KEPT[b, i])) for b in range(SIDE) for i in range(SIDE)]
TO_PLANE = [(line, plane) for plane, line in TO_LINE]
BY_CORE = np.array(
    [[2 * z + (c + k) % 2 for k in range(2) for z in range(SIDE // 2)] for c in range(SIDE)], np.int32
)
KEEPER_BY_CORE = np.take_along_axis(KEEPER, BY_CORE, axis=1)

f32, bf16 = jnp.float32, jnp.bfloat16


def kernel_call(body, outs, args, scratch=(), flops=0, prefetch=0):
    vmem = pl.BlockSpec(memory_space=pltpu.VMEM)
    smem = pl.BlockSpec(memory_space=pltpu.SMEM)
    size = sum(a.size * a.dtype.itemsize for a in args)
    return pl.pallas_call(
        body,
        out_shape=outs,
        in_specs=[smem] * prefetch + [vmem] * (len(args) - prefetch),
        out_specs=jax.tree.map(lambda _: vmem, outs),
        scratch_shapes=list(scratch),
        compiler_params=pltpu.CompilerParams(vmem_limit_bytes=8 * 1024 * 1024),
        cost_estimate=pl.CostEstimate(flops=flops, bytes_accessed=size, transcendentals=0),
    )(*args)


def shape(*dims, dtype=f32):
    return jax.ShapeDtypeStruct(dims, dtype)


def split(values):
    high = values.astype(bf16)
    low = (values - high.astype(f32)).astype(bf16)
    return high, low


def split_kernel(corr_ref, resp_ref, ch_ref, cl_ref, rh_ref, rl_ref):
    @pl.loop(0, WIDTH // LANES)
    def _(i):
        rows = pl.ds(pl.multiple_of(i * LANES, LANES), LANES)
        ch_ref[rows, :], cl_ref[rows, :] = split(corr_ref[rows, :])
        rh_ref[rows, :], rl_ref[rows, :] = split(resp_ref[rows, :])


def split_history(hist_corr, hist_resp):
    out = shape(WIDTH, WIDTH, dtype=bf16)
    return kernel_call(split_kernel, (out,) * 4, (hist_corr, hist_resp), flops=WIDTH * WIDTH)


def cross_kernel(order_ref, full_ref, rh_ref, rl_ref, keep_ref, give_ref, lhs_ref):
    half = SIDE // 2
    for slot in range(0, SIDE, 2):
        pair = [full_ref[order_ref[slot + k]] for k in range(2)]
        full = jnp.concatenate([p[:, :WIDTH] for p in pair], axis=0)
        high, low = split(1.5 * full * full)
        lhs_ref[slot * SLICE : (slot + 2) * SLICE] = high
        lhs_ref[ROWS + slot * SLICE : ROWS + (slot + 2) * SLICE] = low
        for k in range(2):
            out_ref = keep_ref if slot < half else give_ref
            out_ref[slot % half + k, :, WIDTH:] = pair[k][:, WIDTH:]
    dims = (((1,), (1,)), ((), ()))

    @pl.loop(0, WIDTH // TILE)
    def _(n):
        at = pl.ds(pl.multiple_of(n * TILE, TILE), TILE)
        both = lax.dot_general(lhs_ref[...], rh_ref[at, :], dims, preferred_element_type=f32)
        low = lax.dot_general(lhs_ref[:ROWS], rl_ref[at, :], dims, preferred_element_type=f32)
        total = (both[:ROWS] + (both[ROWS:] + low)).reshape(SIDE, SLICE, TILE)
        keep_ref[:, :, at] = total[:half]
        give_ref[:, :, at] = total[half:]


def cross_parts(order, full, resp_high, resp_low):
    out = shape(SIDE // 2, SLICE, WIDTH + LANES)
    return kernel_call(
        cross_kernel,
        (out, out),
        (order, full, resp_high, resp_low),
        scratch=(pltpu.VMEM((2 * ROWS, WIDTH), bf16),),
        flops=6 * ROWS * WIDTH * WIDTH,
        prefetch=1,
    )


def memory_kernel(
    order_ref, mine_ref, other_ref, ch_ref, cl_ref, rh_ref, rl_ref, out_ref, lhs_ref
):
    half = ROWS // 2
    for k, ref in enumerate((mine_ref, other_ref)):
        high, low = split(ref[...].reshape(half, WIDTH))
        lhs_ref[k * half : (k + 1) * half] = high
        lhs_ref[ROWS + k * half : ROWS + (k + 1) * half] = low
    for first, high_ref, low_ref in ((0, ch_ref, cl_ref), (WIDTH, rh_ref, rl_ref)):

        @pl.loop(0, WIDTH // TILE)
        def _(n):
            at = pl.ds(pl.multiple_of(n * TILE, TILE), TILE)
            to = pl.ds(pl.multiple_of(first + n * TILE, TILE), TILE)
            both = jnp.dot(lhs_ref[...], high_ref[:, at], preferred_element_type=f32)
            low = jnp.dot(lhs_ref[:ROWS], low_ref[:, at], preferred_element_type=f32)
            total = (both[:ROWS] + (both[ROWS:] + low)).reshape(SIDE, SLICE, TILE)
            for slot in range(SIDE):
                out_ref[order_ref[slot], :, to] = total[slot]


def memory_parts(order, mine, other, corr_high, corr_low, resp_high, resp_low):
    return kernel_call(
        memory_kernel,
        shape(SIDE, SLICE, 2 * WIDTH),
        (order, mine, other, corr_high, corr_low, resp_high, resp_low),
        scratch=(pltpu.VMEM((2 * ROWS, WIDTH), bf16),),
        flops=12 * ROWS * WIDTH * WIDTH,
        prefetch=1,
    )


def energy_and_terms(corr, resp):
    energy = 3.0 * corr * resp
    slope = 1.5 * corr * corr
    terms = jnp.sum(energy * corr + slope * resp, axis=-1, keepdims=True)
    return energy, jnp.broadcast_to(terms, corr.shape[:-1] + (LANES,))


def advance(pieces, cross, corr, resp):
    sums = jnp.sum(pieces, axis=0)
    memory_corr = sums[:, :WIDTH]
    memory_resp = sums[:, WIDTH:]
    multiplier = heat_reservoir_warmth + COEFFICIENT * cross[:, WIDTH : WIDTH + 1]
    return (
        corr + step_size * (COEFFICIENT * (memory_corr + cross[:, :WIDTH]) - multiplier * corr),
        resp + step_size * (COEFFICIENT * memory_resp - multiplier * resp),
    )


def advance_kernel(pieces_ref, cross_ref, corr_ref, resp_ref, c_ref, r_ref, e_ref, copies_ref):
    corr, resp = advance(pieces_ref[...], cross_ref[...], corr_ref[...], resp_ref[...])
    c_ref[...] = corr
    r_ref[...] = resp
    e_ref[...], terms = energy_and_terms(corr, resp)
    for j in range(SIDE):
        copies_ref[j, :, :WIDTH] = corr
        copies_ref[j, :, WIDTH:] = terms


def last_kernel(pieces_ref, cross_ref, corr_ref, resp_ref, copies_ref):
    corr, resp = advance(pieces_ref[...], cross_ref[...], corr_ref[...], resp_ref[...])
    for j in range(SIDE):
        copies_ref[j, :, :WIDTH] = corr
        copies_ref[j, :, WIDTH:] = resp


def unpack_kernel(keeper_ref, pieces_ref, corr_ref, resp_ref):
    for j in range(SIDE):
        piece = pieces_ref[keeper_ref[j]]
        corr_ref[j] = piece[:, :WIDTH]
        resp_ref[j] = piece[:, WIDTH:]


def swap(values):
    return lax.ppermute(values, "core", [(0, 1), (1, 0)])


def to_line(piece):
    return lax.ppermute(piece, ALL, TO_LINE)


def to_plane(piece):
    return lax.ppermute(piece, ALL, TO_PLANE)


def body(hist_corr, hist_resp, row_corr, row_resp):
    col = 2 * lax.axis_index("z") + lax.axis_index("core")

    def mine_of(table):
        return lax.dynamic_index_in_dim(jnp.asarray(table), col, keepdims=False)

    order = mine_of(KEEPER_BY_CORE)
    row_corr = row_corr.reshape(SIDE, SLICE, WIDTH)
    row_resp = row_resp.reshape(SIDE, SLICE, WIDTH)
    kept = lax.dynamic_index_in_dim(mine_of(KEPT), lax.axis_index(ROW), keepdims=False)
    corr = lax.dynamic_index_in_dim(row_corr, kept, keepdims=False)
    resp = lax.dynamic_index_in_dim(row_resp, kept, keepdims=False)
    energy, _ = energy_and_terms(corr, resp)
    _, terms = energy_and_terms(row_corr, row_resp)
    full = jnp.concatenate([row_corr, terms], axis=2)
    corr_high, corr_low, resp_high, resp_low = split_history(hist_corr, hist_resp)
    piece = shape(SLICE, WIDTH)
    for block_index in range(BLOCKS):
        if block_index:
            full = lax.all_to_all(copies, ROW, 0, 0, tiled=True)
        energy = to_line(energy)
        mine = lax.all_to_all(
            jnp.broadcast_to(energy[None], (SIDE // 2, SLICE, WIDTH)), "z", 0, 0, tiled=True
        )
        other = swap(mine)
        keep, give = cross_parts(
            order if block_index else mine_of(BY_CORE), full, resp_high, resp_low
        )
        cross = lax.all_to_all(keep + swap(give), "z", 0, 0, tiled=True)
        cross = to_plane(jnp.sum(cross, axis=0))
        parts = memory_parts(order, mine, other, corr_high, corr_low, resp_high, resp_low)
        pieces = lax.all_to_all(parts, ROW, 0, 0, tiled=True)
        if block_index < BLOCKS - 1:
            corr, resp, energy, copies = kernel_call(
                advance_kernel,
                (piece, piece, piece, shape(SIDE, SLICE, WIDTH + LANES)),
                (pieces, cross, corr, resp),
            )
        else:
            copies = kernel_call(
                last_kernel, shape(SIDE, SLICE, 2 * WIDTH), (pieces, cross, corr, resp)
            )
    final = lax.all_to_all(copies, ROW, 0, 0, tiled=True)
    out = shape(SIDE, SLICE, WIDTH)
    final_corr, final_resp = kernel_call(
        unpack_kernel, (out, out), (mine_of(KEEPER), final), prefetch=1
    )
    return (final_corr.reshape(ROWS, WIDTH), final_resp.reshape(ROWS, WIDTH))


def solution(mesh):
    split_mesh = Mesh(mesh.devices.reshape(4, 4, 8, 2), ALL)
    times = ("z", "core")
    in_specs = (P(ROW, times), P(ROW, times), P(None, times), P(None, times))
    out_specs = (P(None, times), P(None, times))
    return jax.shard_map(
        body, mesh=split_mesh, in_specs=in_specs, out_specs=out_specs, check_vma=False
    )
```

```python
import functools
import math

import jax
import jax.numpy as jnp
import numpy as np
from jax import lax
from jax.experimental import pallas as pl
from jax.experimental.pallas import tpu as pltpu
from jax.sharding import Mesh
from jax.sharding import PartitionSpec as P

HIST = 16384
BLOCKS = 4
SIDE = 16
SLICE = 8
ROWS = SIDE * SLICE
WIDTH = 1024
LANES = 128
TILE = 256
SMALL, LARGE = 8 * 2**20, 42 * 2**20
HELD = 12
TILES = WIDTH // TILE
COEFFICIENT = 1.0 / math.sqrt(HIST)

step_size = 0.2
heat_reservoir_warmth = 0.6

ROW = ("y", "x")
ALL = ("y", "x", "z", "core")


def around(a, b, size):
    return min((a - b) % size, (b - a) % size)


def pairs_of(b):
    def plane(i):
        return around(i // 4, b // 4, 4) + around(i % 4, b % 4, 4)

    rows = sorted(range(SIDE), key=lambda i: (-plane(i), i))
    cols = sorted(range(SIDE), key=lambda j: (around(j // 2, b // 2, 8), j))
    return dict(zip(rows, cols))


PAIRS = [pairs_of(b) for b in range(SIDE)]
KEPT = np.array([[PAIRS[b][i] for i in range(SIDE)] for b in range(SIDE)], np.int32)
KEEPER = np.argsort(KEPT, axis=1).astype(np.int32)
TO_LINE = [(i * SIDE + b, b * SIDE + int(KEPT[b, i])) for b in range(SIDE) for i in range(SIDE)]
TO_PLANE = [(line, plane) for plane, line in TO_LINE]
BY_CORE = np.array(
    [[2 * z + (c + k) % 2 for k in range(2) for z in range(SIDE // 2)] for c in range(SIDE)], np.int32
)
KEEPER_BY_CORE = np.take_along_axis(KEEPER, BY_CORE, axis=1)

f32, bf16 = jnp.float32, jnp.bfloat16


def kernel_call(body, outs, args, scratch=(), flops=0, scalars=0, history=0, far=False):
    vmem = pl.BlockSpec(memory_space=pltpu.VMEM)
    smem = pl.BlockSpec(memory_space=pltpu.SMEM)
    hbm = pl.BlockSpec(memory_space=pltpu.HBM)
    size = sum(a.size * a.dtype.itemsize for a in args)
    return pl.pallas_call(
        body,
        out_shape=outs,
        in_specs=[smem] * scalars + [vmem] * (len(args) - scalars - history) + [hbm] * history,
        out_specs=jax.tree.map(lambda _: hbm if far else vmem, outs),
        scratch_shapes=list(scratch),
        compiler_params=pltpu.CompilerParams(vmem_limit_bytes=(LARGE if history or far else SMALL)),
        cost_estimate=pl.CostEstimate(flops=flops, bytes_accessed=size, transcendentals=0),
    )(*args)


def shape(*dims, dtype=f32):
    return jax.ShapeDtypeStruct(dims, dtype)


def split(values):
    high = values.astype(bf16)
    low = (values - high.astype(f32)).astype(bf16)
    return high, low


def split_kernel(corr, resp, out, read_ref, held_ref, read_sems, sems):
    reads, copies = [], []
    for n in range(TILES):
        for k, history in enumerate((corr, resp)):
            at = pl.ds(n * TILE, TILE)
            reads.append(
                pltpu.make_async_copy(
                    history.at[at], read_ref.at[k, at], read_sems.at[k * TILES + n]
                )
            )
            reads[-1].start()
    for n in range(TILES):
        at = slice(n * TILE, (n + 1) * TILE)
        for k in range(2):
            reads[2 * n + k].wait()
            held_ref[2 * k, at], held_ref[2 * k + 1, at] = split(read_ref[k, at])
        copies.append(pltpu.make_async_copy(held_ref.at[:, at], out.at[pl.ds(0, 4), at], sems.at[n]))
        copies[-1].start()
    for copy in copies:
        copy.wait()


def split_history(hist_corr, hist_resp):
    return kernel_call(
        split_kernel,
        shape(HELD, WIDTH, WIDTH, dtype=bf16),
        (hist_corr, hist_resp),
        scratch=(
            pltpu.VMEM((2, WIDTH, WIDTH), f32),
            pltpu.VMEM((4, WIDTH, WIDTH), bf16),
            pltpu.SemaphoreType.DMA((2 * TILES,)),
            pltpu.SemaphoreType.DMA((TILES,)),
        ),
        flops=WIDTH * WIDTH,
        history=2,
        far=True,
    )


def cross_kernel(order_ref, full_ref, history, keep_ref, give_ref, lhs_ref, held_ref, sems):
    copies = []
    for n in range(TILES):
        at = pl.ds(n * TILE, TILE)
        copies.append(
            pltpu.make_async_copy(history.at[pl.ds(2, 2), at], held_ref.at[:, at], sems.at[n])
        )
        copies[-1].start()
    half = SIDE // 2
    for slot in range(0, SIDE, 2):
        pair = [full_ref[order_ref[slot + k]] for k in range(2)]
        full = jnp.concatenate([p[:, :WIDTH] for p in pair], axis=0)
        high, low = split(1.5 * full * full)
        lhs_ref[slot * SLICE : (slot + 2) * SLICE] = high
        lhs_ref[ROWS + slot * SLICE : ROWS + (slot + 2) * SLICE] = low
        for k in range(2):
            out_ref = keep_ref if slot < half else give_ref
            out_ref[slot % half + k, :, WIDTH:] = pair[k][:, WIDTH:]
    dims = (((1,), (1,)), ((), ()))
    for n in range(TILES):
        copies[n].wait()
        at = slice(n * TILE, (n + 1) * TILE)
        both = lax.dot_general(lhs_ref[...], held_ref[0, at], dims, preferred_element_type=f32)
        low = lax.dot_general(lhs_ref[:ROWS], held_ref[1, at], dims, preferred_element_type=f32)
        total = (both[:ROWS] + (both[ROWS:] + low)).reshape(SIDE, SLICE, TILE)
        keep_ref[:, :, at] = total[:half]
        give_ref[:, :, at] = total[half:]


def cross_parts(order, full, history):
    out = shape(SIDE // 2, SLICE, WIDTH + LANES)
    return kernel_call(
        cross_kernel,
        (out, out),
        (order, full, history),
        scratch=(
            pltpu.VMEM((2 * ROWS, WIDTH), bf16),
            pltpu.VMEM((2, WIDTH, WIDTH), bf16),
            pltpu.SemaphoreType.DMA((TILES,)),
        ),
        flops=6 * ROWS * WIDTH * WIDTH,
        scalars=1,
        history=1,
    )


def memory_kernel(
    order_ref, mine_ref, other_ref, history, out_hbm, lhs_ref, held_ref, out_ref, sems, out_sems
):
    copies = []
    for k in range(2):
        for n in range(TILES):
            at = pl.ds(n * TILE, TILE)
            parts = pl.ds(2 * k, 2)
            copies.append(
                pltpu.make_async_copy(
                    history.at[parts, :, at], held_ref.at[parts, :, at], sems.at[k * TILES + n]
                )
            )
            copies[-1].start()
    half = ROWS // 2
    for k, ref in enumerate((mine_ref, other_ref)):
        high, low = split(ref[...].reshape(half, WIDTH))
        lhs_ref[k * half : (k + 1) * half] = high
        lhs_ref[ROWS + k * half : ROWS + (k + 1) * half] = low
    results = []
    for k in range(2):
        for n in range(TILES):
            copies[k * TILES + n].wait()
            at = slice(n * TILE, (n + 1) * TILE)
            both = jnp.dot(lhs_ref[...], held_ref[2 * k, :, at], preferred_element_type=f32)
            low = jnp.dot(lhs_ref[:ROWS], held_ref[2 * k + 1, :, at], preferred_element_type=f32)
            total = (both[:ROWS] + (both[ROWS:] + low)).reshape(SIDE, SLICE, TILE)
            to = k * WIDTH + n * TILE
            for slot in range(SIDE):
                out_ref[order_ref[slot], :, to : to + TILE] = total[slot]
            to = pl.ds(to, TILE)
            results.append(
                pltpu.make_async_copy(
                    out_ref.at[:, :, to], out_hbm.at[:, :, to], out_sems.at[k * TILES + n]
                )
            )
            results[-1].start()
    for copy in results:
        copy.wait()


def memory_parts(order, mine, other, history):
    return kernel_call(
        memory_kernel,
        shape(SIDE, SLICE, 2 * WIDTH),
        (order, mine, other, history),
        scratch=(
            pltpu.VMEM((2 * ROWS, WIDTH), bf16),
            pltpu.VMEM((4, WIDTH, WIDTH), bf16),
            pltpu.VMEM((SIDE, SLICE, 2 * WIDTH), f32),
            pltpu.SemaphoreType.DMA((2 * TILES,)),
            pltpu.SemaphoreType.DMA((2 * TILES,)),
        ),
        flops=12 * ROWS * WIDTH * WIDTH,
        scalars=1,
        history=1,
        far=True,
    )


def energy_and_terms(corr, resp):
    energy = 3.0 * corr * resp
    slope = 1.5 * corr * corr
    terms = jnp.sum(energy * corr + slope * resp, axis=-1, keepdims=True)
    return energy, jnp.broadcast_to(terms, corr.shape[:-1] + (LANES,))


def advance(pieces, cross, corr, resp):
    sums = jnp.sum(pieces, axis=0)
    memory_corr = sums[:, :WIDTH]
    memory_resp = sums[:, WIDTH:]
    multiplier = heat_reservoir_warmth + COEFFICIENT * cross[:, WIDTH : WIDTH + 1]
    return (
        corr + step_size * (COEFFICIENT * (memory_corr + cross[:, :WIDTH]) - multiplier * corr),
        resp + step_size * (COEFFICIENT * memory_resp - multiplier * resp),
    )


def advance_kernel(pieces_ref, cross_ref, corr_ref, resp_ref, c_ref, r_ref, e_ref, copies_ref):
    corr, resp = advance(pieces_ref[...], cross_ref[...], corr_ref[...], resp_ref[...])
    c_ref[...] = corr
    r_ref[...] = resp
    e_ref[...], terms = energy_and_terms(corr, resp)
    for j in range(SIDE):
        copies_ref[j, :, :WIDTH] = corr
        copies_ref[j, :, WIDTH:] = terms


def last_kernel(pieces_ref, cross_ref, corr_ref, resp_ref, copies_ref):
    corr, resp = advance(pieces_ref[...], cross_ref[...], corr_ref[...], resp_ref[...])
    for j in range(SIDE):
        copies_ref[j, :, :WIDTH] = corr
        copies_ref[j, :, WIDTH:] = resp


def unpack_kernel(keeper_ref, pieces_ref, corr_ref, resp_ref):
    for j in range(SIDE):
        piece = pieces_ref[keeper_ref[j]]
        corr_ref[j] = piece[:, :WIDTH]
        resp_ref[j] = piece[:, WIDTH:]


def swap(values):
    return lax.ppermute(values, "core", [(0, 1), (1, 0)])


def to_line(piece):
    return lax.ppermute(piece, ALL, TO_LINE)


def to_plane(piece):
    return lax.ppermute(piece, ALL, TO_PLANE)


def spread_kernel(energy_ref, copies_ref):
    for z in range(SIDE // 2):
        copies_ref[z] = energy_ref[...]


def pass_kernel(cross_ref, out_ref):
    out_ref[...] = cross_ref[...]


def body(hist_corr, hist_resp, row_corr, row_resp):
    col = 2 * lax.axis_index("z") + lax.axis_index("core")

    def mine_of(table):
        return lax.dynamic_index_in_dim(jnp.asarray(table), col, keepdims=False)

    order = mine_of(KEEPER_BY_CORE)
    row_corr = row_corr.reshape(SIDE, SLICE, WIDTH)
    row_resp = row_resp.reshape(SIDE, SLICE, WIDTH)
    kept = lax.dynamic_index_in_dim(mine_of(KEPT), lax.axis_index(ROW), keepdims=False)
    corr = lax.dynamic_index_in_dim(row_corr, kept, keepdims=False)
    resp = lax.dynamic_index_in_dim(row_resp, kept, keepdims=False)
    energy, _ = energy_and_terms(corr, resp)
    _, terms = energy_and_terms(row_corr, row_resp)
    full = jnp.concatenate([row_corr, terms], axis=2)
    history = split_history(hist_corr, hist_resp)
    piece = shape(SLICE, WIDTH)
    for block_index in range(BLOCKS):
        if block_index:
            full = lax.all_to_all(copies, ROW, 0, 0, tiled=True)
        energy = to_line(energy)
        mine = lax.all_to_all(
            jnp.broadcast_to(energy[None], (SIDE // 2, SLICE, WIDTH)), "z", 0, 0, tiled=True
        )
        other = swap(mine)
        keep, give = cross_parts(
            order if block_index else mine_of(BY_CORE), full, history
        )
        cross = lax.all_to_all(keep + swap(give), "z", 0, 0, tiled=True)
        cross = to_plane(jnp.sum(cross, axis=0))
        parts = memory_parts(order, mine, other, history)
        pieces = lax.all_to_all(parts, ROW, 0, 0, tiled=True)
        if block_index < BLOCKS - 1:
            corr, resp, energy, copies = kernel_call(
                advance_kernel,
                (piece, piece, piece, shape(SIDE, SLICE, WIDTH + LANES)),
                (pieces, cross, corr, resp),
            )
        else:
            copies = kernel_call(
                last_kernel, shape(SIDE, SLICE, 2 * WIDTH), (pieces, cross, corr, resp)
            )
    final = lax.all_to_all(copies, ROW, 0, 0, tiled=True)
    out = shape(SIDE, SLICE, WIDTH)
    final_corr, final_resp = kernel_call(
        unpack_kernel, (out, out), (mine_of(KEEPER), final), scalars=1
    )
    return (final_corr.reshape(ROWS, WIDTH), final_resp.reshape(ROWS, WIDTH))


def solution(mesh):
    split_mesh = Mesh(mesh.devices.reshape(4, 4, 8, 2), ALL)
    times = ("z", "core")
    in_specs = (P(ROW, times), P(ROW, times), P(None, times), P(None, times))
    out_specs = (P(None, times), P(None, times))
    return jax.shard_map(
        body, mesh=split_mesh, in_specs=in_specs, out_specs=out_specs, check_vma=False
    )
```

```python
import functools
import math

import jax
import jax.numpy as jnp
import numpy as np
from jax import lax
from jax.experimental import pallas as pl
from jax.experimental.pallas import tpu as pltpu
from jax.sharding import Mesh
from jax.sharding import PartitionSpec as P

HIST = 16384
BLOCKS = 4
SIDE = 16
SLICE = 8
ROWS = SIDE * SLICE
WIDTH = 1024
LANES = 128
TILE = 512
SMALL, LARGE = 8 * 2**20, 42 * 2**20
HELD = 12
TILES = WIDTH // TILE
COEFFICIENT = 1.0 / math.sqrt(HIST)

step_size = 0.2
heat_reservoir_warmth = 0.6

ROW = ("y", "x")
ALL = ("y", "x", "z", "core")


def around(a, b, size):
    return min((a - b) % size, (b - a) % size)


def pairs_of(b):
    def plane(i):
        return around(i // 4, b // 4, 4) + around(i % 4, b % 4, 4)

    rows = sorted(range(SIDE), key=lambda i: (-plane(i), i))
    cols = sorted(range(SIDE), key=lambda j: (around(j // 2, b // 2, 8), j))
    return dict(zip(rows, cols))


PAIRS = [pairs_of(b) for b in range(SIDE)]
KEPT = np.array([[PAIRS[b][i] for i in range(SIDE)] for b in range(SIDE)], np.int32)
KEEPER = np.argsort(KEPT, axis=1).astype(np.int32)
TO_LINE = [(i * SIDE + b, b * SIDE + int(KEPT[b, i])) for b in range(SIDE) for i in range(SIDE)]
TO_PLANE = [(line, plane) for plane, line in TO_LINE]
BY_CORE = np.array(
    [[2 * z + (c + k) % 2 for k in range(2) for z in range(SIDE // 2)] for c in range(SIDE)], np.int32
)
KEEPER_BY_CORE = np.take_along_axis(KEEPER, BY_CORE, axis=1)

f32, bf16 = jnp.float32, jnp.bfloat16


def kernel_call(body, outs, args, scratch=(), flops=0, scalars=0, history=0, far=False, limit=SMALL):
    vmem = pl.BlockSpec(memory_space=pltpu.VMEM)
    smem = pl.BlockSpec(memory_space=pltpu.SMEM)
    hbm = pl.BlockSpec(memory_space=pltpu.HBM)
    size = sum(a.size * a.dtype.itemsize for a in args)
    return pl.pallas_call(
        body,
        out_shape=outs,
        in_specs=[smem] * scalars + [vmem] * (len(args) - scalars - history) + [hbm] * history,
        out_specs=jax.tree.map(lambda _: hbm if far else vmem, outs),
        scratch_shapes=list(scratch),
        compiler_params=pltpu.CompilerParams(vmem_limit_bytes=limit),
        cost_estimate=pl.CostEstimate(flops=flops, bytes_accessed=size, transcendentals=0),
    )(*args)


def shape(*dims, dtype=f32):
    return jax.ShapeDtypeStruct(dims, dtype)


def split(values):
    high = values.astype(bf16)
    low = (values - high.astype(f32)).astype(bf16)
    return high, low


def split_kernel(corr, resp, out, read_ref, held_ref, read_sems, sems):
    reads, copies = [], []
    for n in range(TILES):
        for k, history in enumerate((corr, resp)):
            at = pl.ds(n * TILE, TILE)
            reads.append(
                pltpu.make_async_copy(
                    history.at[at], read_ref.at[k, at], read_sems.at[k * TILES + n]
                )
            )
            reads[-1].start()
    for n in range(TILES):
        at = slice(n * TILE, (n + 1) * TILE)
        for k in range(2):
            reads[2 * n + k].wait()
            held_ref[2 * k, at], held_ref[2 * k + 1, at] = split(read_ref[k, at])
        copies.append(pltpu.make_async_copy(held_ref.at[:, at], out.at[pl.ds(0, 4), at], sems.at[n]))
        copies[-1].start()
    for copy in copies:
        copy.wait()


def split_history(hist_corr, hist_resp):
    return kernel_call(
        split_kernel,
        shape(HELD, WIDTH, WIDTH, dtype=bf16),
        (hist_corr, hist_resp),
        scratch=(
            pltpu.VMEM((2, WIDTH, WIDTH), f32),
            pltpu.VMEM((4, WIDTH, WIDTH), bf16),
            pltpu.SemaphoreType.DMA((2 * TILES,)),
            pltpu.SemaphoreType.DMA((TILES,)),
        ),
        flops=WIDTH * WIDTH,
        history=2,
        far=True,
        limit=58 * 2**20,
    )


def cross_kernel(order_ref, full_ref, history, keep_ref, give_ref, lhs_ref, held_ref, sems):
    copies = []
    for n in range(TILES):
        at = pl.ds(n * TILE, TILE)
        copies.append(
            pltpu.make_async_copy(history.at[pl.ds(2, 2), at], held_ref.at[:, at], sems.at[n])
        )
        copies[-1].start()
    half = SIDE // 2
    for slot in range(0, SIDE, 2):
        pair = [full_ref[order_ref[slot + k]] for k in range(2)]
        full = jnp.concatenate([p[:, :WIDTH] for p in pair], axis=0)
        high, low = split(1.5 * full * full)
        lhs_ref[slot * SLICE : (slot + 2) * SLICE] = high
        lhs_ref[ROWS + slot * SLICE : ROWS + (slot + 2) * SLICE] = low
        for k in range(2):
            out_ref = keep_ref if slot < half else give_ref
            out_ref[slot % half + k, :, WIDTH:] = pair[k][:, WIDTH:]
    dims = (((1,), (1,)), ((), ()))
    for n in range(TILES):
        copies[n].wait()
        at = slice(n * TILE, (n + 1) * TILE)
        both = lax.dot_general(lhs_ref[...], held_ref[0, at], dims, preferred_element_type=f32)
        low = lax.dot_general(lhs_ref[:ROWS], held_ref[1, at], dims, preferred_element_type=f32)
        total = (both[:ROWS] + (both[ROWS:] + low)).reshape(SIDE, SLICE, TILE)
        keep_ref[:, :, at] = total[:half]
        give_ref[:, :, at] = total[half:]


def cross_parts(order, full, history):
    out = shape(SIDE // 2, SLICE, WIDTH + LANES)
    return kernel_call(
        cross_kernel,
        (out, out),
        (order, full, history),
        scratch=(
            pltpu.VMEM((2 * ROWS, WIDTH), bf16),
            pltpu.VMEM((2, WIDTH, WIDTH), bf16),
            pltpu.SemaphoreType.DMA((TILES,)),
        ),
        flops=6 * ROWS * WIDTH * WIDTH,
        scalars=1,
        history=1,
        limit=LARGE,
    )


def memory_kernel(
    order_ref, mine_ref, other_ref, history, out_hbm, lhs_ref, held_ref, out_ref, sems, out_sems
):
    copies = []
    for k in range(2):
        for n in range(TILES):
            at = pl.ds(n * TILE, TILE)
            parts = pl.ds(2 * k, 2)
            copies.append(
                pltpu.make_async_copy(
                    history.at[parts, :, at], held_ref.at[parts, :, at], sems.at[k * TILES + n]
                )
            )
            copies[-1].start()
    half = ROWS // 2
    for k, ref in enumerate((mine_ref, other_ref)):
        high, low = split(ref[...].reshape(half, WIDTH))
        lhs_ref[k * half : (k + 1) * half] = high
        lhs_ref[ROWS + k * half : ROWS + (k + 1) * half] = low
    results = []
    for k in range(2):
        for n in range(TILES):
            copies[k * TILES + n].wait()
            at = slice(n * TILE, (n + 1) * TILE)
            both = jnp.dot(lhs_ref[...], held_ref[2 * k, :, at], preferred_element_type=f32)
            low = jnp.dot(lhs_ref[:ROWS], held_ref[2 * k + 1, :, at], preferred_element_type=f32)
            total = (both[:ROWS] + (both[ROWS:] + low)).reshape(SIDE, SLICE, TILE)
            to = k * WIDTH + n * TILE
            for slot in range(SIDE):
                out_ref[order_ref[slot], :, to : to + TILE] = total[slot]
            to = pl.ds(to, TILE)
            results.append(
                pltpu.make_async_copy(
                    out_ref.at[:, :, to], out_hbm.at[:, :, to], out_sems.at[k * TILES + n]
                )
            )
            results[-1].start()
    for copy in results:
        copy.wait()


def memory_parts(order, mine, other, history):
    return kernel_call(
        memory_kernel,
        shape(SIDE, SLICE, 2 * WIDTH),
        (order, mine, other, history),
        scratch=(
            pltpu.VMEM((2 * ROWS, WIDTH), bf16),
            pltpu.VMEM((4, WIDTH, WIDTH), bf16),
            pltpu.VMEM((SIDE, SLICE, 2 * WIDTH), f32),
            pltpu.SemaphoreType.DMA((2 * TILES,)),
            pltpu.SemaphoreType.DMA((2 * TILES,)),
        ),
        flops=12 * ROWS * WIDTH * WIDTH,
        scalars=1,
        history=1,
        far=True,
        limit=LARGE,
    )


def energy_and_terms(corr, resp):
    energy = 3.0 * corr * resp
    slope = 1.5 * corr * corr
    terms = jnp.sum(energy * corr + slope * resp, axis=-1, keepdims=True)
    return energy, jnp.broadcast_to(terms, corr.shape[:-1] + (LANES,))


def advance(pieces, cross, corr, resp):
    sums = jnp.sum(pieces, axis=0)
    memory_corr = sums[:, :WIDTH]
    memory_resp = sums[:, WIDTH:]
    multiplier = heat_reservoir_warmth + COEFFICIENT * cross[:, WIDTH : WIDTH + 1]
    return (
        corr + step_size * (COEFFICIENT * (memory_corr + cross[:, :WIDTH]) - multiplier * corr),
        resp + step_size * (COEFFICIENT * memory_resp - multiplier * resp),
    )


def advance_kernel(pieces_ref, cross_ref, corr_ref, resp_ref, c_ref, r_ref, e_ref, copies_ref):
    corr, resp = advance(pieces_ref[...], cross_ref[...], corr_ref[...], resp_ref[...])
    c_ref[...] = corr
    r_ref[...] = resp
    e_ref[...], terms = energy_and_terms(corr, resp)
    for j in range(SIDE):
        copies_ref[j, :, :WIDTH] = corr
        copies_ref[j, :, WIDTH:] = terms


def last_kernel(pieces_ref, cross_ref, corr_ref, resp_ref, copies_ref):
    corr, resp = advance(pieces_ref[...], cross_ref[...], corr_ref[...], resp_ref[...])
    for j in range(SIDE):
        copies_ref[j, :, :WIDTH] = corr
        copies_ref[j, :, WIDTH:] = resp


def unpack_kernel(keeper_ref, pieces_ref, corr_ref, resp_ref):
    for j in range(SIDE):
        piece = pieces_ref[keeper_ref[j]]
        corr_ref[j] = piece[:, :WIDTH]
        resp_ref[j] = piece[:, WIDTH:]


def swap(values):
    return lax.ppermute(values, "core", [(0, 1), (1, 0)])


def to_line(piece):
    return lax.ppermute(piece, ALL, TO_LINE)


def to_plane(piece):
    return lax.ppermute(piece, ALL, TO_PLANE)


def spread_kernel(energy_ref, copies_ref):
    for z in range(SIDE // 2):
        copies_ref[z] = energy_ref[...]


def pass_kernel(cross_ref, out_ref):
    out_ref[...] = cross_ref[...]


def body(hist_corr, hist_resp, row_corr, row_resp):
    col = 2 * lax.axis_index("z") + lax.axis_index("core")

    def mine_of(table):
        return lax.dynamic_index_in_dim(jnp.asarray(table), col, keepdims=False)

    order = mine_of(KEEPER_BY_CORE)
    row_corr = row_corr.reshape(SIDE, SLICE, WIDTH)
    row_resp = row_resp.reshape(SIDE, SLICE, WIDTH)
    kept = lax.dynamic_index_in_dim(mine_of(KEPT), lax.axis_index(ROW), keepdims=False)
    corr = lax.dynamic_index_in_dim(row_corr, kept, keepdims=False)
    resp = lax.dynamic_index_in_dim(row_resp, kept, keepdims=False)
    energy, _ = energy_and_terms(corr, resp)
    _, terms = energy_and_terms(row_corr, row_resp)
    full = jnp.concatenate([row_corr, terms], axis=2)
    history = split_history(hist_corr, hist_resp)
    piece = shape(SLICE, WIDTH)
    for block_index in range(BLOCKS):
        if block_index:
            full = lax.all_to_all(copies, ROW, 0, 0, tiled=True)
        energy = to_line(energy)
        mine = lax.all_to_all(
            jnp.broadcast_to(energy[None], (SIDE // 2, SLICE, WIDTH)), "z", 0, 0, tiled=True
        )
        other = swap(mine)
        keep, give = cross_parts(
            order if block_index else mine_of(BY_CORE), full, history
        )
        cross = lax.all_to_all(keep + swap(give), "z", 0, 0, tiled=True)
        cross = to_plane(jnp.sum(cross, axis=0))
        parts = memory_parts(order, mine, other, history)
        pieces = lax.all_to_all(parts, ROW, 0, 0, tiled=True)
        if block_index < BLOCKS - 1:
            corr, resp, energy, copies = kernel_call(
                advance_kernel,
                (piece, piece, piece, shape(SIDE, SLICE, WIDTH + LANES)),
                (pieces, cross, corr, resp),
            )
        else:
            copies = kernel_call(
                last_kernel, shape(SIDE, SLICE, 2 * WIDTH), (pieces, cross, corr, resp)
            )
    final = lax.all_to_all(copies, ROW, 0, 0, tiled=True)
    out = shape(SIDE, SLICE, WIDTH)
    final_corr, final_resp = kernel_call(
        unpack_kernel, (out, out), (mine_of(KEEPER), final), scalars=1
    )
    return (final_corr.reshape(ROWS, WIDTH), final_resp.reshape(ROWS, WIDTH))


def solution(mesh):
    split_mesh = Mesh(mesh.devices.reshape(4, 4, 8, 2), ALL)
    times = ("z", "core")
    in_specs = (P(ROW, times), P(ROW, times), P(None, times), P(None, times))
    out_specs = (P(None, times), P(None, times))
    return jax.shard_map(
        body, mesh=split_mesh, in_specs=in_specs, out_specs=out_specs, check_vma=False
    )
```

```python
import functools
import math

import jax
import jax.numpy as jnp
import numpy as np
from jax import lax
from jax.experimental import pallas as pl
from jax.experimental.pallas import tpu as pltpu
from jax.sharding import Mesh
from jax.sharding import PartitionSpec as P

HIST = 16384
BLOCKS = 4
SIDE = 16
SLICE = 8
ROWS = SIDE * SLICE
WIDTH = 1024
LANES = 128
TILE = 512
SMALL, LARGE = 8 * 2**20, 42 * 2**20
HELD = 12
TILES = WIDTH // TILE
COEFFICIENT = 1.0 / math.sqrt(HIST)

step_size = 0.2
heat_reservoir_warmth = 0.6

ROW = ("y", "x")
ALL = ("y", "x", "z", "core")


def around(a, b, size):
    return min((a - b) % size, (b - a) % size)


def pairs_of(b):
    def plane(i):
        return around(i // 4, b // 4, 4) + around(i % 4, b % 4, 4)

    rows = sorted(range(SIDE), key=lambda i: (-plane(i), i))
    cols = sorted(range(SIDE), key=lambda j: (around(j // 2, b // 2, 8), j))
    return dict(zip(rows, cols))


PAIRS = [pairs_of(b) for b in range(SIDE)]
KEPT = np.array([[PAIRS[b][i] for i in range(SIDE)] for b in range(SIDE)], np.int32)
KEEPER = np.argsort(KEPT, axis=1).astype(np.int32)
TO_LINE = [(i * SIDE + b, b * SIDE + int(KEPT[b, i])) for b in range(SIDE) for i in range(SIDE)]
TO_PLANE = [(line, plane) for plane, line in TO_LINE]
BY_CORE = np.array(
    [[2 * z + (c + k) % 2 for k in range(2) for z in range(SIDE // 2)] for c in range(SIDE)], np.int32
)
KEEPER_BY_CORE = np.take_along_axis(KEEPER, BY_CORE, axis=1)

f32, bf16 = jnp.float32, jnp.bfloat16


def kernel_call(body, outs, args, scratch=(), flops=0, scalars=0, history=0, far=False, limit=SMALL):
    vmem = pl.BlockSpec(memory_space=pltpu.VMEM)
    smem = pl.BlockSpec(memory_space=pltpu.SMEM)
    hbm = pl.BlockSpec(memory_space=pltpu.HBM)
    size = sum(a.size * a.dtype.itemsize for a in args)
    return pl.pallas_call(
        body,
        out_shape=outs,
        in_specs=[smem] * scalars + [vmem] * (len(args) - scalars - history) + [hbm] * history,
        out_specs=jax.tree.map(lambda _: hbm if far else vmem, outs),
        scratch_shapes=list(scratch),
        compiler_params=pltpu.CompilerParams(vmem_limit_bytes=limit),
        cost_estimate=pl.CostEstimate(flops=flops, bytes_accessed=size, transcendentals=0),
    )(*args)


def shape(*dims, dtype=f32):
    return jax.ShapeDtypeStruct(dims, dtype)


def split(values):
    high = values.astype(bf16)
    low = (values - high.astype(f32)).astype(bf16)
    return high, low


def split_kernel(corr, resp, out, read_ref, held_ref, read_sems, sems):
    reads, copies = [], []
    for n in range(TILES):
        for k, history in enumerate((corr, resp)):
            at = pl.ds(n * TILE, TILE)
            reads.append(
                pltpu.make_async_copy(
                    history.at[at], read_ref.at[k, at], read_sems.at[k * TILES + n]
                )
            )
            reads[-1].start()
    for n in range(TILES):
        at = slice(n * TILE, (n + 1) * TILE)
        for k in range(2):
            reads[2 * n + k].wait()
            held_ref[2 * k, at], held_ref[2 * k + 1, at] = split(read_ref[k, at])
        copies.append(pltpu.make_async_copy(held_ref.at[:, at], out.at[pl.ds(0, 4), at], sems.at[n]))
        copies[-1].start()
    for copy in copies:
        copy.wait()


def split_history(hist_corr, hist_resp):
    return kernel_call(
        split_kernel,
        shape(HELD, WIDTH, WIDTH, dtype=bf16),
        (hist_corr, hist_resp),
        scratch=(
            pltpu.VMEM((2, WIDTH, WIDTH), f32),
            pltpu.VMEM((4, WIDTH, WIDTH), bf16),
            pltpu.SemaphoreType.DMA((2 * TILES,)),
            pltpu.SemaphoreType.DMA((TILES,)),
        ),
        flops=WIDTH * WIDTH,
        history=2,
        far=True,
        limit=58 * 2**20,
    )


def cross_kernel(order_ref, full_ref, history, keep_ref, give_ref, lhs_ref, held_ref, sems):
    copies = []
    for n in range(TILES):
        at = pl.ds(n * TILE, TILE)
        copies.append(
            pltpu.make_async_copy(history.at[pl.ds(2, 2), at], held_ref.at[:, at], sems.at[n])
        )
        copies[-1].start()
    half = SIDE // 2
    for slot in range(0, SIDE, 2):
        pair = [full_ref[order_ref[slot + k]] for k in range(2)]
        full = jnp.concatenate([p[:, :WIDTH] for p in pair], axis=0)
        high, low = split(1.5 * full * full)
        lhs_ref[slot * SLICE : (slot + 2) * SLICE] = high
        lhs_ref[ROWS + slot * SLICE : ROWS + (slot + 2) * SLICE] = low
        for k in range(2):
            out_ref = keep_ref if slot < half else give_ref
            out_ref[slot % half + k, :, WIDTH:] = pair[k][:, WIDTH:]
    dims = (((1,), (1,)), ((), ()))
    for n in range(TILES):
        copies[n].wait()
        at = slice(n * TILE, (n + 1) * TILE)
        both = lax.dot_general(lhs_ref[...], held_ref[0, at], dims, preferred_element_type=f32)
        low = lax.dot_general(lhs_ref[:ROWS], held_ref[1, at], dims, preferred_element_type=f32)
        total = (both[:ROWS] + (both[ROWS:] + low)).reshape(SIDE, SLICE, TILE)
        keep_ref[:, :, at] = total[:half]
        give_ref[:, :, at] = total[half:]


def cross_parts(order, full, history):
    out = shape(SIDE // 2, SLICE, WIDTH + LANES)
    return kernel_call(
        cross_kernel,
        (out, out),
        (order, full, history),
        scratch=(
            pltpu.VMEM((2 * ROWS, WIDTH), bf16),
            pltpu.VMEM((2, WIDTH, WIDTH), bf16),
            pltpu.SemaphoreType.DMA((TILES,)),
        ),
        flops=6 * ROWS * WIDTH * WIDTH,
        scalars=1,
        history=1,
        limit=LARGE,
    )


def memory_kernel(
    order_ref, mine_ref, other_ref, history, out_hbm, lhs_ref, held_ref, out_ref, sems, out_sems
):
    copies = []
    for k in range(2):
        for n in range(TILES):
            at = pl.ds(n * TILE, TILE)
            parts = pl.ds(2 * k, 2)
            copies.append(
                pltpu.make_async_copy(
                    history.at[parts, :, at], held_ref.at[parts, :, at], sems.at[k * TILES + n]
                )
            )
            copies[-1].start()
    half = ROWS // 2
    for k, ref in enumerate((mine_ref, other_ref)):
        high, low = split(ref[...].reshape(half, WIDTH))
        lhs_ref[k * half : (k + 1) * half] = high
        lhs_ref[ROWS + k * half : ROWS + (k + 1) * half] = low
    results = []
    for k in range(2):
        for n in range(TILES):
            copies[k * TILES + n].wait()
            at = slice(n * TILE, (n + 1) * TILE)
            both = jnp.dot(lhs_ref[...], held_ref[2 * k, :, at], preferred_element_type=f32)
            low = jnp.dot(lhs_ref[:ROWS], held_ref[2 * k + 1, :, at], preferred_element_type=f32)
            total = (both[:ROWS] + (both[ROWS:] + low)).reshape(SIDE, SLICE, TILE)
            to = k * WIDTH + n * TILE
            for slot in range(SIDE):
                out_ref[order_ref[slot], :, to : to + TILE] = total[slot]
            to = pl.ds(to, TILE)
            results.append(
                pltpu.make_async_copy(
                    out_ref.at[:, :, to], out_hbm.at[:, :, to], out_sems.at[k * TILES + n]
                )
            )
            results[-1].start()
    for copy in results:
        copy.wait()


def memory_parts(order, mine, other, history):
    return kernel_call(
        memory_kernel,
        shape(SIDE, SLICE, 2 * WIDTH),
        (order, mine, other, history),
        scratch=(
            pltpu.VMEM((2 * ROWS, WIDTH), bf16),
            pltpu.VMEM((4, WIDTH, WIDTH), bf16),
            pltpu.VMEM((SIDE, SLICE, 2 * WIDTH), f32),
            pltpu.SemaphoreType.DMA((2 * TILES,)),
            pltpu.SemaphoreType.DMA((2 * TILES,)),
        ),
        flops=12 * ROWS * WIDTH * WIDTH,
        scalars=1,
        history=1,
        far=True,
        limit=LARGE,
    )


def energy_and_terms(corr, resp):
    energy = 3.0 * corr * resp
    slope = 1.5 * corr * corr
    terms = jnp.sum(energy * corr + slope * resp, axis=-1, keepdims=True)
    return energy, jnp.broadcast_to(terms, corr.shape[:-1] + (LANES,))


def advance(pieces, cross, corr, resp):
    sums = jnp.sum(pieces, axis=0)
    memory_corr = sums[:, :WIDTH]
    memory_resp = sums[:, WIDTH:]
    multiplier = heat_reservoir_warmth + COEFFICIENT * cross[:, WIDTH : WIDTH + 1]
    return (
        corr + step_size * (COEFFICIENT * (memory_corr + cross[:, :WIDTH]) - multiplier * corr),
        resp + step_size * (COEFFICIENT * memory_resp - multiplier * resp),
    )


def first_kernel(place_ref, kept_ref, all_corr, all_resp, c_ref, r_ref, e_ref, full_ref):
    kept = kept_ref[place_ref[0], place_ref[1]]
    corr, resp = all_corr[kept], all_resp[kept]
    c_ref[...] = corr
    r_ref[...] = resp
    e_ref[...], _ = energy_and_terms(corr, resp)
    for j in range(SIDE):
        full_ref[j, :, :WIDTH] = all_corr[j]
        _, full_ref[j, :, WIDTH:] = energy_and_terms(all_corr[j], all_resp[j])


def advance_kernel(pieces_ref, cross_ref, corr_ref, resp_ref, c_ref, r_ref, e_ref, copies_ref):
    corr, resp = advance(pieces_ref[...], cross_ref[...], corr_ref[...], resp_ref[...])
    c_ref[...] = corr
    r_ref[...] = resp
    e_ref[...], terms = energy_and_terms(corr, resp)
    for j in range(SIDE):
        copies_ref[j, :, :WIDTH] = corr
        copies_ref[j, :, WIDTH:] = terms


def last_kernel(pieces_ref, cross_ref, corr_ref, resp_ref, copies_ref):
    corr, resp = advance(pieces_ref[...], cross_ref[...], corr_ref[...], resp_ref[...])
    for j in range(SIDE):
        copies_ref[j, :, :WIDTH] = corr
        copies_ref[j, :, WIDTH:] = resp


def unpack_kernel(keeper_ref, pieces_ref, corr_ref, resp_ref):
    for j in range(SIDE):
        piece = pieces_ref[keeper_ref[j]]
        corr_ref[j] = piece[:, :WIDTH]
        resp_ref[j] = piece[:, WIDTH:]


def swap(values):
    return lax.ppermute(values, "core", [(0, 1), (1, 0)])


def to_line(piece):
    return lax.ppermute(piece, ALL, TO_LINE)


def to_plane(piece):
    return lax.ppermute(piece, ALL, TO_PLANE)


def spread_kernel(energy_ref, copies_ref):
    for z in range(SIDE // 2):
        copies_ref[z] = energy_ref[...]


def pass_kernel(cross_ref, out_ref):
    out_ref[...] = cross_ref[...]


def body(hist_corr, hist_resp, row_corr, row_resp):
    col = 2 * lax.axis_index("z") + lax.axis_index("core")

    def mine_of(table):
        return lax.dynamic_index_in_dim(jnp.asarray(table), col, keepdims=False)

    order = mine_of(KEEPER_BY_CORE)
    row_corr = row_corr.reshape(SIDE, SLICE, WIDTH)
    row_resp = row_resp.reshape(SIDE, SLICE, WIDTH)
    piece = shape(SLICE, WIDTH)
    place = jnp.stack([col, lax.axis_index(ROW)])
    corr, resp, energy, full = kernel_call(
        first_kernel,
        (piece, piece, piece, shape(SIDE, SLICE, WIDTH + LANES)),
        (place, jnp.asarray(KEPT), row_corr, row_resp),
        scalars=2,
    )
    history = split_history(hist_corr, hist_resp)
    piece = shape(SLICE, WIDTH)
    for block_index in range(BLOCKS):
        if block_index:
            full = lax.all_to_all(copies, ROW, 0, 0, tiled=True)
        energy = to_line(energy)
        mine = lax.all_to_all(
            jnp.broadcast_to(energy[None], (SIDE // 2, SLICE, WIDTH)), "z", 0, 0, tiled=True
        )
        other = swap(mine)
        keep, give = cross_parts(
            order if block_index else mine_of(BY_CORE), full, history
        )
        cross = lax.all_to_all(keep + swap(give), "z", 0, 0, tiled=True)
        cross = to_plane(jnp.sum(cross, axis=0))
        parts = memory_parts(order, mine, other, history)
        pieces = lax.all_to_all(parts, ROW, 0, 0, tiled=True)
        if block_index < BLOCKS - 1:
            corr, resp, energy, copies = kernel_call(
                advance_kernel,
                (piece, piece, piece, shape(SIDE, SLICE, WIDTH + LANES)),
                (pieces, cross, corr, resp),
            )
        else:
            copies = kernel_call(
                last_kernel, shape(SIDE, SLICE, 2 * WIDTH), (pieces, cross, corr, resp)
            )
    final = lax.all_to_all(copies, ROW, 0, 0, tiled=True)
    out = shape(SIDE, SLICE, WIDTH)
    final_corr, final_resp = kernel_call(
        unpack_kernel, (out, out), (mine_of(KEEPER), final), scalars=1
    )
    return (final_corr.reshape(ROWS, WIDTH), final_resp.reshape(ROWS, WIDTH))


def solution(mesh):
    split_mesh = Mesh(mesh.devices.reshape(4, 4, 8, 2), ALL)
    times = ("z", "core")
    in_specs = (P(ROW, times), P(ROW, times), P(None, times), P(None, times))
    out_specs = (P(None, times), P(None, times))
    return jax.shard_map(
        body, mesh=split_mesh, in_specs=in_specs, out_specs=out_specs, check_vma=False
    )
```
